32 devices in a mesh: parts: 2 (over y), tm: 4 (over z), space: 2 (over x), spin: 2 (over core).
Axes of the slice: x: 2, y: 2, z: 4, core: 2. Of those that a mesh axis runs over, the one named last changes fastest.
Arguments:
- eigenvectors: float32 [2, 8, 3, 512, 256], P(None, ('parts', 'tm'), None, ('space', 'spin')), parts along dimension 1, may hold values from -0.25 to 0.25
- displaced: float32 [2, 3, 8, 3, 512, 256], P(None, None, ('parts', 'tm'), None, ('space', 'spin')), parts along dimension 2, may hold values from -0.25 to 0.25
- perambulators: float32 [2, 8, 4, 256, 256], P(None, 'parts', 'spin', 'space', 'tm'), parts along dimension 1, may hold values from -6 to 6
- gamma_values: float32 [2, 4, 4, 4], replicated, may hold values from -4 to 4
- spin_pattern: int32 [4, 4, 4], replicated, may hold values 0 or 1
- directions: int32 [4], replicated, may hold values from 0 to 2, as said below
- momenta: int32 [4], replicated, may hold values from 0 to 3
Outputs:
- products: float32 [2, 4, 8, 4, 256, 256], P(None, None, ('parts', 'tm'), 'spin', 'space'), parts along dimension 2
The draws below stay inside these ranges and needn't reach their ends.
There are 2 independent parts, one for each index of `parts`. The reference program is written for one: setup_inputs(seed, part) draws one part's arguments, and reference() takes and returns one part's arrays. A program takes and returns all parts, laid end to end along the dimension named above; an argument that names none is the same for every part. Nothing has to cross between parts.
Inputs may be any that keep to these rules, and one draw needn't show every extreme that they name: Every one of the 3 directions is named by some operator.
All inputs are finite; a program needn't handle non-finite values.
Results may differ from the reference program's by a relative error of at most 0.0001.
Values sent between devices are 32-bit elements; how exact they have to be, the bound alone decides.
A program may use at most 64 MiB of HBM per device.

```python
import math
import jax
import jax.numpy as jnp
from jax import lax

K = 256
SRC = 256
NSPIN = 4
NOP = 4
NDIR = 3
NMOM = 4
NT = 4
NSITES = 512
PLANE = 256
LZ = 2


def draw_directions(key, part):
    first = jax.random.permutation(jax.random.fold_in(key, 11), NDIR).astype(jnp.int32)
    extra = jax.random.randint(jax.random.fold_in(key, 12), (NOP - NDIR,), 0, NDIR).astype(jnp.int32)
    return jnp.concatenate([first, extra]).astype(jnp.int32)


def touch_ends(result, own_key, least, top_value):
    place = [jax.random.randint(jax.random.fold_in(own_key, axis), (), 0, length) for axis, length in enumerate(result.shape)]
    longest = result.shape.index(max(result.shape))
    neighbour = place[:longest] + [(place[longest] + 1) % result.shape[longest]] + place[longest + 1:]
    return result.at[tuple(place)].set(least).at[tuple(neighbour)].set(top_value)


def block_scale(key, dims, split, least, largest):
    factor_of, own = 1.0, jax.random.fold_in(key, 6)
    for dim, shards_of in split:
        draws = jnp.exp(jax.random.uniform(jax.random.fold_in(own, dim), (shards_of,), jnp.float32, least / len(split), largest / len(split)))
        factor_of = factor_of * jnp.repeat(draws, dims[dim] // shards_of).reshape([-1 if axis == dim else 1 for axis in range(len(dims))])
    return factor_of


def scatter_about(key, dims, width, bound, cuts=(), kind=jnp.bfloat16):
    gain = block_scale(key, dims, cuts, -0.22, 0.18) if cuts else 1.0
    values = jax.random.normal(key, dims, jnp.float32) * width * gain
    return jnp.minimum(jnp.maximum(values, -bound), bound).astype(kind)


def setup_inputs(seed: int = 0, part: int = 0) -> dict:
    key_list = jax.random.split(jax.random.key(seed), 8)
    part_keys = jax.random.split(jax.random.fold_in(key_list[7], part), 8)
    eigenvectors = scatter_about(part_keys[0], (2, NT, 3, NSITES, K), NSITES ** -0.5, 0.25, ((1, 4), (3, 4)), jnp.float32)
    displaced = scatter_about(part_keys[1], (2, NDIR, NT, 3, NSITES, K), NSITES ** -0.5, 0.25, ((2, 4), (4, 4)), jnp.float32)
    perambulators = scatter_about(part_keys[2], (2, NT, NSPIN, K, SRC), 1.0, 6.0, ((2, 2), (3, 2), (4, 4)), jnp.float32)
    gamma_values = scatter_about(key_list[3], (2, NOP, NSPIN, NSPIN), 0.7, 4.0, (), jnp.float32)
    spin_pattern = touch_ends((jax.random.randint(key_list[4], (NOP, NSPIN, NSPIN), 0, 2) < 1).astype(jnp.int32), jax.random.fold_in(key_list[4], 1), 0, 1)
    directions = draw_directions(jax.random.fold_in(key_list[7], 71), part)
    momenta = touch_ends(jax.random.randint(key_list[6], (NOP,), 0, NMOM), jax.random.fold_in(key_list[6], 1), 0, NMOM - 1).astype(jnp.int32)
    return {"eigenvectors": eigenvectors, "displaced": displaced, "perambulators": perambulators, "gamma_values": gamma_values, "spin_pattern": spin_pattern, "directions": directions, "momenta": momenta}


highest = lax.Precision.HIGHEST


def reference(eigenvectors, displaced, perambulators, gamma_values, spin_pattern, directions, momenta):
    sites = jnp.arange(NSITES, dtype=jnp.int32)
    third = sites // PLANE
    angles = ((momenta[:, None] * third[None, :]) % LZ).astype(jnp.float32) * (2.0 * math.pi / LZ)
    cosine = jnp.cos(angles)
    sine = jnp.sin(angles)
    spin_matrix = gamma_values * spin_pattern.astype(jnp.float32)[None]

    def per_time(tslice):
        vectors = lax.dynamic_index_in_dim(eigenvectors, tslice, 1, keepdims=False)
        left = vectors.reshape(-1, K)
        rows = []
        for operator in range(NOP):
            moved = lax.dynamic_index_in_dim(displaced, directions[operator], 1, keepdims=False)
            moved = lax.dynamic_index_in_dim(moved, tslice, 1, keepdims=False)
            cos_row = cosine[operator][:, None]
            sin_row = sine[operator][:, None]
            real_w = cos_row * moved[0] + sin_row * moved[1]
            imag_w = cos_row * moved[1] - sin_row * moved[0]
            right = jnp.concatenate([jnp.stack([real_w, imag_w]), jnp.stack([imag_w, -real_w])], axis=-1).reshape(-1, 2 * K)
            elem = lax.dot_general(left, right, (((0,), (0,)), ((), ())), precision=highest, preferred_element_type=jnp.float32)
            rows.append(elem.reshape(K, 2, K))
        elementals = jnp.stack(rows)
        real_e = elementals[:, :, 0]
        imag_e = elementals[:, :, 1]
        peram = lax.dynamic_index_in_dim(perambulators, tslice, 1, keepdims=False)
        real_q = jnp.einsum('oab,bls->oals', spin_matrix[0], peram[0], precision=highest) - jnp.einsum('oab,bls->oals', spin_matrix[1], peram[1], precision=highest)
        imag_q = jnp.einsum('oab,bls->oals', spin_matrix[0], peram[1], precision=highest) + jnp.einsum('oab,bls->oals', spin_matrix[1], peram[0], precision=highest)
        real_r = jnp.einsum('okl,oals->oaks', real_e, real_q, precision=highest) - jnp.einsum('okl,oals->oaks', imag_e, imag_q, precision=highest)
        imag_r = jnp.einsum('okl,oals->oaks', real_e, imag_q, precision=highest) + jnp.einsum('okl,oals->oaks', imag_e, real_q, precision=highest)
        return jnp.stack([real_r, imag_r])

    results = lax.map(per_time, jnp.arange(NT, dtype=jnp.int32))
    return jnp.transpose(results, (1, 2, 0, 3, 4, 5))
```

```python
import functools
import math

import jax
import jax.numpy as jnp
import numpy as np
from jax import lax
from jax.experimental import pallas as pl
from jax.experimental.pallas import tpu as pltpu
from jax.sharding import PartitionSpec as P

MESH = pl.DeviceIdType.MESH
f32 = jnp.float32
bf16 = jnp.bfloat16


def split(value):
    high = value.astype(bf16)
    return high, (value - high.astype(f32)).astype(bf16)


def dot3(a_high, a_low, b_high, b_low):
    dot = functools.partial(jnp.dot, preferred_element_type=f32)
    return dot(a_high, b_high) + (dot(a_high, b_low) + dot(a_low, b_high))


def turn(value, groups, by):
    if by == 0:
        return value
    width = value.shape[-1]
    cut = width // groups * by
    if width % 128 == 0:
        return pltpu.roll(value, width - cut, 1)
    return jnp.concatenate([value[:, cut:], value[:, :cut]], axis=1)


def table(index, values):
    result = f32(values[0])
    for j in range(1, len(values)):
        result = jnp.where(index == j, f32(values[j]), result)
    return result


def exchange(
    n_tm, n_space, n_spin,
    vec_hbm, dis_hbm, per_hbm, gamma, pattern, directions, momenta,
    y_ref,
    vec, dis, per, lhs_h, lhs_l, part, part_in, g_out, g_in,
    stage, slots, elem, elem_h, elem_l, w_h, w_l,
    load_sem, z_send, z_recv, x_send, x_recv, s_send, s_recv,
    gs_send, gs_recv, gx_send, gx_recv, e_send, e_recv,
):
    n_op = gamma.shape[1]
    n_dir = dis_hbm.shape[1]
    nb = per_hbm.shape[2]
    rows = part.shape[4]
    width = part.shape[5]
    l_rows = slots.shape[4]
    lanes = slots.shape[5]
    z = lax.axis_index("tm")
    x = lax.axis_index("space")
    c = lax.axis_index("spin")
    other = 1 - c

    def tm_peer(d):
        return {"tm": lax.rem(z + d, n_tm)}

    def x_peer(e):
        return {"space": lax.rem(x + e, n_space)}

    sibling = {"spin": other}

    loads = [pltpu.make_async_copy(per_hbm, per, load_sem.at[0])]
    loads.append(pltpu.make_async_copy(vec_hbm.at[:, 0], vec, load_sem.at[1]))
    for k in range(n_dir):
        loads.append(pltpu.make_async_copy(dis_hbm.at[:, k, 0], dis.at[k], load_sem.at[2 + k]))
    for load in loads:
        load.start()

    peers = [tm_peer(d) for d in range(1, n_tm)] + [x_peer(e) for e in range(1, n_space)] + [sibling]
    barrier = pltpu.get_barrier_semaphore()
    for peer in peers:
        pl.semaphore_signal(barrier, inc=1, device_id=peer, device_id_type=MESH)
    pl.semaphore_wait(barrier, len(peers))

    sent = []

    def send(src, dst, send_sem, recv_sem, peer):
        copy = pltpu.make_async_remote_copy(
            src_ref=src, dst_ref=dst, send_sem=send_sem, recv_sem=recv_sem,
            device_id=peer, device_id_type=MESH,
        )
        copy.start()
        sent.append(copy)
        return copy

    def packed(tslice, reim):
        return jnp.concatenate([per[reim, tslice, b] for b in range(nb)], axis=1)

    from_sibling = {}
    from_x = {}
    from_z = {}

    def forward_sibling(e, d):
        from_sibling[e, d] = send(
            slots.at[e, d, c], slots.at[e, d, c], s_send.at[e, d], s_recv.at[e, d], sibling
        )

    def forward_x(d):
        for e in range(1, n_space):
            from_x[e, d] = send(
                slots.at[0, d, c], slots.at[e, d, c], x_send.at[e, d], x_recv.at[e, d], x_peer(e)
            )

    loads[0].wait()
    for reim in range(2):
        slots[0, 0, c, reim] = packed(z, reim)
    forward_x(0)
    order = sorted(range(1, n_tm), key=lambda d: min(d, n_tm - d))
    for d in order:
        for reim in range(2):
            stage[d, reim] = packed(lax.rem(z + d, n_tm), reim)
        from_z[d] = send(stage.at[d], slots.at[0, d, c], z_send.at[d], z_recv.at[d], tm_peer(d))
    forward_sibling(0, 0)

    depth = lhs_h.shape[1]
    half = depth // 2
    loads[1].wait()
    turned = vec[...].reshape(depth, width).T
    high, low = split(turned)
    for ref, value in ((lhs_h, high), (lhs_l, low)):
        ref[:width] = value
        ref[width:, :half] = -value[:, half:]
        ref[width:, half:] = value[:, :half]
    from_part = []
    to_x = {}

    def reduce_part(k):
        from_part[k].wait_recv()
        for e in range(n_space):
            dest = lax.rem(x + e, n_space)
            total = part[k, c, dest] + part_in[k, dest]
            if e == 0:
                g_in[k, 0] = total
            else:
                g_out[k, e] = total
                to_x[k, e] = send(
                    g_out.at[k, e], g_in.at[k, e], gx_send.at[k, e], gx_recv.at[k, e], x_peer(e)
                )

    for k in range(n_dir):
        loads[2 + k].wait()
        r_high, r_low = split(dis[k].reshape(depth, width))
        sums = dot3(lhs_h[...], lhs_l[...], r_high, r_low)
        for xb in range(n_space):
            for cb in range(n_spin):
                first = (xb * n_spin + cb) * rows
                for reim in range(2):
                    start = reim * width + first
                    part[k, cb, xb, reim] = sums[start : start + rows]
        from_part.append(
            send(part.at[k, other], part_in.at[k], gs_send.at[k], gs_recv.at[k], sibling)
        )
        if k > 0:
            reduce_part(k - 1)
    reduce_part(n_dir - 1)

    lane = lax.broadcasted_iota(jnp.int32, (1, lanes), 1)
    cols = lanes // nb

    def mix(e, d):
        first = pl.multiple_of(lax.rem(x + (n_space - e), n_space) * l_rows, l_rows)

        def one(o, carry):
            q_re = jnp.zeros((l_rows, lanes), f32)
            q_im = jnp.zeros((l_rows, lanes), f32)
            for cb in range(n_spin):
                real = slots[e, d, cb, 0]
                imag = slots[e, d, cb, 1]
                for r in range(nb):
                    factors = []
                    for reim in range(2):
                        vector = jnp.zeros((1, lanes), f32)
                        for a in range(nb):
                            b = cb * nb + (a + r) % nb
                            row = c * nb + a
                            value = gamma[reim, o, row, b] * pattern[o, row, b].astype(f32)
                            if a == 0:
                                vector = jnp.full((1, lanes), value)
                            else:
                                vector = jnp.where(lane >= a * cols, value, vector)
                        factors.append(vector)
                    re_r = turn(real, nb, r)
                    im_r = turn(imag, nb, r)
                    q_re += factors[0] * re_r - factors[1] * im_r
                    q_im += factors[0] * im_r + factors[1] * re_r
            w_high, w_low = split(jnp.concatenate([q_re, q_im], axis=1))
            w_h[d, o, pl.ds(first, l_rows)] = w_high
            w_l[d, o, pl.ds(first, l_rows)] = w_low
            return carry

        lax.fori_loop(0, n_op, one, 0)

    def take_x(d):
        for e in range(1, n_space):
            from_x[e, d].wait_recv()
            forward_sibling(e, d)

    for d in order:
        from_z[d].wait_recv()
        forward_x(d)
        forward_sibling(0, d)
    take_x(0)
    for d in [0] + order:
        from_sibling[0, d].wait_recv()
        mix(0, d)
    for e in range(1, n_space):
        from_sibling[e, 0].wait_recv()
        mix(e, 0)

    for copy in to_x.values():
        copy.wait_recv()
    angles = np.arange(n_space, dtype=np.float32) * np.float32(2.0 * math.pi / n_space)
    cosines = [float(v) for v in np.cos(angles)]
    sines = [float(v) for v in np.sin(angles)]
    for o in range(n_op):
        e_re = jnp.zeros((rows, width), f32)
        e_im = jnp.zeros((rows, width), f32)
        way = directions[o]
        for e in range(n_space):
            plane = lax.rem(x + (n_space - e), n_space)
            step = lax.rem(momenta[o] * plane, n_space)
            cos_s = table(step, cosines)
            sin_s = table(step, sines)
            g_re = g_in[way, e, 0]
            g_im = g_in[way, e, 1]
            e_re += cos_s * g_re + sin_s * g_im
            e_im += cos_s * g_im - sin_s * g_re
        elem[c, o, 0] = e_re
        elem[c, o, 1] = e_im
    elem_copy = send(elem.at[c], elem.at[c], e_send.at[0], e_recv.at[0], sibling)
    k_rows = n_spin * rows
    elem_copy.wait_recv()
    for o in range(n_op):
        for reim in range(2):
            value = jnp.concatenate([elem[cb, o, reim] for cb in range(n_spin)], axis=0)
            high, low = split(value)
            elem_h[o, reim * k_rows : (reim + 1) * k_rows] = high
            elem_l[o, reim * k_rows : (reim + 1) * k_rows] = low

    def multiply(d):
        owner = lax.rem(z + (n_tm - d), n_tm)

        def one(o, carry):
            m = dot3(elem_h[o], elem_l[o], w_h[d, o], w_l[d, o])
            y_ref[0, o, owner] = m[:k_rows, :lanes] - m[k_rows:, lanes:]
            y_ref[1, o, owner] = m[:k_rows, lanes:] + m[k_rows:, :lanes]
            return carry

        lax.fori_loop(0, n_op, one, 0)

    multiply(0)
    before = None
    for d in order + [None]:
        if d is not None:
            take_x(d)
        if before is not None:
            for e in range(1, n_space):
                from_sibling[e, before].wait_recv()
                mix(e, before)
            multiply(before)
        before = d

    for copy in sent:
        copy.wait_send()


def arrange(y_ref, out_ref):
    owners = y_ref.shape[2]
    nb = out_ref.shape[3]
    cols = y_ref.shape[4] // nb
    for reim in range(y_ref.shape[0]):
        for a in range(nb):
            out_ref[reim, 0, 0, a] = jnp.concatenate(
                [y_ref[reim, 0, owner, :, a * cols : (a + 1) * cols] for owner in range(owners)], axis=1
            )


def local(n_tm, n_space, n_spin, eigenvectors, displaced, perambulators, gamma_values, spin_pattern, directions, momenta):
    _, _, colours, sites, width = eigenvectors.shape
    n_dir = displaced.shape[1]
    n_op = gamma_values.shape[1]
    _, _, nb, l_rows, cols = perambulators.shape
    rows = width // (n_space * n_spin)
    k_rows = width // n_space
    lanes = nb * cols
    depth = 2 * colours * sites
    dma = pltpu.SemaphoreType.DMA
    smem = pl.BlockSpec(memory_space=pltpu.SMEM)
    hbm = pl.BlockSpec(memory_space=pl.ANY)
    y = pl.pallas_call(
        functools.partial(exchange, n_tm, n_space, n_spin),
        out_shape=jax.ShapeDtypeStruct((2, n_op, n_tm, k_rows, lanes), f32),
        in_specs=[hbm, hbm, hbm, smem, smem, smem, smem],
        out_specs=pl.BlockSpec(memory_space=pltpu.VMEM),
        scratch_shapes=[
            pltpu.VMEM((2, colours, sites, width), f32),
            pltpu.VMEM((n_dir, 2, colours, sites, width), f32),
            pltpu.VMEM(perambulators.shape, f32),
            pltpu.VMEM((2 * width, depth), bf16),
            pltpu.VMEM((2 * width, depth), bf16),
            pltpu.VMEM((n_dir, n_spin, n_space, 2, rows, width), f32),
            pltpu.VMEM((n_dir, n_space, 2, rows, width), f32),
            pltpu.VMEM((n_dir, n_space, 2, rows, width), f32),
            pltpu.VMEM((n_dir, n_space, 2, rows, width), f32),
            pltpu.VMEM((n_tm, 2, l_rows, lanes), f32),
            pltpu.VMEM((n_space, n_tm, n_spin, 2, l_rows, lanes), f32),
            pltpu.VMEM((n_spin, n_op, 2, rows, width), f32),
            pltpu.VMEM((n_op, 2 * k_rows, width), bf16),
            pltpu.VMEM((n_op, 2 * k_rows, width), bf16),
            pltpu.VMEM((n_tm, n_op, width, 2 * lanes), bf16),
            pltpu.VMEM((n_tm, n_op, width, 2 * lanes), bf16),
            dma((2 + n_dir,)),
            dma((n_tm,)), dma((n_tm,)),
            dma((n_space, n_tm)), dma((n_space, n_tm)),
            dma((n_space, n_tm)), dma((n_space, n_tm)),
            dma((n_dir,)), dma((n_dir,)),
            dma((n_dir, n_space)), dma((n_dir, n_space)),
            dma((1,)), dma((1,)),
        ],
        compiler_params=pltpu.CompilerParams(
            collective_id=0, has_side_effects=True, vmem_limit_bytes=44 * 2**20
        ),
        name="exchange_and_multiply",
    )(eigenvectors, displaced, perambulators, gamma_values, spin_pattern, directions, momenta)
    return pl.pallas_call(
        arrange,
        grid=(n_op,),
        out_shape=jax.ShapeDtypeStruct((2, n_op, 1, nb, k_rows, n_tm * cols), f32),
        in_specs=[pl.BlockSpec((2, 1, n_tm, k_rows, lanes), lambda o: (0, o, 0, 0, 0))],
        out_specs=pl.BlockSpec((2, 1, 1, nb, k_rows, n_tm * cols), lambda o: (0, o, 0, 0, 0, 0)),
        compiler_params=pltpu.CompilerParams(vmem_limit_bytes=16 * 2**20),
        name="arrange",
    )(y)


def solution(mesh):
    in_specs = (
        P(None, ("parts", "tm"), None, ("space", "spin"), None),
        P(None, None, ("parts", "tm"), None, ("space", "spin"), None),
        P(None, "parts", "spin", "space", "tm"),
        P(),
        P(),
        P(),
        P(),
    )
    out_specs = P(None, None, ("parts", "tm"), "spin", "space", None)
    run = functools.partial(local, mesh.shape["tm"], mesh.shape["space"], mesh.shape["spin"])
    return jax.shard_map(run, mesh=mesh, in_specs=in_specs, out_specs=out_specs, check_vma=False)
```

```python
import functools
import math

import jax
import jax.numpy as jnp
import numpy as np
from jax import lax
from jax.experimental import pallas as pl
from jax.experimental.pallas import tpu as pltpu
from jax.sharding import PartitionSpec as P

MESH = pl.DeviceIdType.MESH
f32 = jnp.float32
bf16 = jnp.bfloat16


def split(value):
    high = value.astype(bf16)
    return high, (value - high.astype(f32)).astype(bf16)


def dot3(a_high, a_low, b_high, b_low, contract=0):
    dims = (((1,), (contract,)), ((), ()))
    dot = functools.partial(lax.dot_general, dimension_numbers=dims, preferred_element_type=f32)
    return dot(a_high, b_high) + (dot(a_high, b_low) + dot(a_low, b_high))


def table(index, values):
    result = f32(values[0])
    for j in range(1, len(values)):
        result = jnp.where(index == j, f32(values[j]), result)
    return result


def exchange(
    n_tm, n_space, n_spin,
    vec_hbm, dis_hbm, per_hbm, gamma_hbm, pattern_hbm, directions_hbm, momenta_hbm,
    out_ref,
    gamma, pattern, directions, momenta,
    vec, dis, lhs_h, lhs_l, part, part_in, g_out, g_in,
    slots, elem, elem_h, elem_l, w_h, w_l,
    load_sem, z_send, z_recv, x_send, x_recv, s_send, s_recv,
    gs_send, gs_recv, gx_send, gx_recv, e_send, e_recv,
):
    n_op = gamma.shape[1]
    n_dir = dis_hbm.shape[1]
    nb = per_hbm.shape[2]
    rows = part.shape[4]
    width = part.shape[5]
    cols = per_hbm.shape[3]
    lanes = nb * cols
    z = lax.axis_index("tm")
    x = lax.axis_index("space")
    c = lax.axis_index("spin")
    other = 1 - c

    def tm_peer(d):
        return {"tm": lax.rem(z + d, n_tm)}

    def x_peer(e):
        return {"space": lax.rem(x + e, n_space)}

    sibling = {"spin": other}

    own = pltpu.make_async_copy(per_hbm.at[:, z], slots.at[0, 0, c], load_sem.at[0])
    loads = [pltpu.make_async_copy(vec_hbm.at[:, 0], vec, load_sem.at[1])]
    for k in range(n_dir):
        loads.append(pltpu.make_async_copy(dis_hbm.at[:, k, 0], dis.at[k], load_sem.at[2 + k]))
    small = [(gamma_hbm, gamma), (pattern_hbm, pattern), (directions_hbm, directions), (momenta_hbm, momenta)]
    tables = [
        pltpu.make_async_copy(src, dst, load_sem.at[2 + n_dir + k]) for k, (src, dst) in enumerate(small)
    ]
    for load in loads + [own] + tables:
        load.start()

    peers = [tm_peer(d) for d in range(1, n_tm)] + [x_peer(e) for e in range(1, n_space)] + [sibling]
    barrier = pltpu.get_barrier_semaphore()
    for peer in peers:
        pl.semaphore_signal(barrier, inc=1, device_id=peer, device_id_type=MESH)
    pl.semaphore_wait(barrier, len(peers))

    sent = []

    def send(src, dst, send_sem, recv_sem, peer):
        copy = pltpu.make_async_remote_copy(
            src_ref=src, dst_ref=dst, send_sem=send_sem, recv_sem=recv_sem,
            device_id=peer, device_id_type=MESH,
        )
        copy.start()
        sent.append(copy)
        return copy

    from_sibling = {}
    from_x = {}
    from_z = {}

    def forward_sibling(e, d, src=None):
        from_sibling[e, d] = send(
            slots.at[e, d, c] if src is None else src, slots.at[e, d, c], s_send.at[e, d], s_recv.at[e, d], sibling
        )

    def forward_x(d, src=None):
        for e in range(1, n_space):
            from_x[e, d] = send(
                slots.at[0, d, c] if src is None else src, slots.at[e, d, c], x_send.at[e, d], x_recv.at[e, d], x_peer(e)
            )

    forward_x(0, per_hbm.at[:, z])
    order = sorted(range(1, n_tm), key=lambda d: min(d, n_tm - d))
    for d in order:
        from_z[d] = send(
            per_hbm.at[:, lax.rem(z + d, n_tm)], slots.at[0, d, c], z_send.at[d], z_recv.at[d], tm_peer(d)
        )
    forward_sibling(0, 0, per_hbm.at[:, z])

    depth = lhs_h.shape[1]
    half = depth // 2
    loads[0].wait()
    turned = vec[...].reshape(depth, width).T
    high, low = split(turned)
    for ref, value in ((lhs_h, high), (lhs_l, low)):
        ref[:width] = value
        ref[width:, :half] = -value[:, half:]
        ref[width:, half:] = value[:, :half]
    from_part = []
    to_x = {}

    def reduce_part(k):
        from_part[k].wait_recv()
        for e in range(n_space):
            dest = lax.rem(x + e, n_space)
            total = part[k, c, dest] + part_in[k, dest]
            if e == 0:
                g_in[k, 0] = total
            else:
                g_out[k, e] = total
                to_x[k, e] = send(
                    g_out.at[k, e], g_in.at[k, e], gx_send.at[k, e], gx_recv.at[k, e], x_peer(e)
                )

    def pass_on(d):
        from_z[d].wait_recv()
        forward_x(d)
        forward_sibling(0, d)

    for k in range(n_dir):
        loads[1 + k].wait()
        r_high, r_low = split(dis[k].reshape(depth, width))
        sums = dot3(lhs_h[...], lhs_l[...], r_high, r_low)
        for xb in range(n_space):
            for cb in range(n_spin):
                first = (xb * n_spin + cb) * rows
                for reim in range(2):
                    start = reim * width + first
                    part[k, cb, xb, reim] = sums[start : start + rows]
        from_part.append(
            send(part.at[k, other], part_in.at[k], gs_send.at[k], gs_recv.at[k], sibling)
        )
        if k > 0:
            reduce_part(k - 1)
        if k == 1:
            pass_on(order[0])
    reduce_part(n_dir - 1)
    for d in order[1:]:
        pass_on(d)

    def mix(e, d):
        block = lax.rem(x + (n_space - e), n_space)

        def one(o, carry):
            for a in range(nb):
                q_re = q_im = None
                row = c * nb + a
                for cb in range(n_spin):
                    for b in range(nb):
                        present = pattern[o, row, cb * nb + b].astype(f32)
                        s_re = gamma[0, o, row, cb * nb + b] * present
                        s_im = gamma[1, o, row, cb * nb + b] * present
                        real = slots[e, d, cb, 0, b]
                        imag = slots[e, d, cb, 1, b]
                        t_re = s_re * real - s_im * imag
                        t_im = s_re * imag + s_im * real
                        q_re = t_re if q_re is None else q_re + t_re
                        q_im = t_im if q_im is None else q_im + t_im
                for reim, value in ((0, q_re), (1, q_im)):
                    high, low = split(value)
                    first = reim * lanes + a * cols
                    w_h[d, o, block, first : first + cols] = high
                    w_l[d, o, block, first : first + cols] = low
            return carry

        lax.fori_loop(0, n_op, one, 0)

    def take_x(d):
        for e in range(1, n_space):
            from_x[e, d].wait_recv()
            forward_sibling(e, d)

    for copy in tables + [own]:
        copy.wait()
    take_x(0)
    for d in [0] + order:
        from_sibling[0, d].wait_recv()
        mix(0, d)
    for e in range(1, n_space):
        from_sibling[e, 0].wait_recv()
        mix(e, 0)

    for copy in to_x.values():
        copy.wait_recv()
    angles = np.arange(n_space, dtype=np.float32) * np.float32(2.0 * math.pi / n_space)
    cosines = [float(v) for v in np.cos(angles)]
    sines = [float(v) for v in np.sin(angles)]
    for o in range(n_op):
        e_re = jnp.zeros((rows, width), f32)
        e_im = jnp.zeros((rows, width), f32)
        way = directions[o]
        for e in range(n_space):
            plane = lax.rem(x + (n_space - e), n_space)
            step = lax.rem(momenta[o] * plane, n_space)
            cos_s = table(step, cosines)
            sin_s = table(step, sines)
            g_re = g_in[way, e, 0]
            g_im = g_in[way, e, 1]
            e_re += cos_s * g_re + sin_s * g_im
            e_im += cos_s * g_im - sin_s * g_re
        elem[c, o, 0] = e_re
        elem[c, o, 1] = e_im
    elem_copy = send(elem.at[c], elem.at[c], e_send.at[0], e_recv.at[0], sibling)
    k_rows = n_spin * rows
    elem_copy.wait_recv()
    for o in range(n_op):
        for reim in range(2):
            value = jnp.concatenate([elem[cb, o, reim] for cb in range(n_spin)], axis=0)
            high, low = split(value)
            elem_h[o, reim * k_rows : (reim + 1) * k_rows] = high
            elem_l[o, reim * k_rows : (reim + 1) * k_rows] = low

    tile = 128
    per_tile = tile // cols
    lane = lax.broadcasted_iota(jnp.int32, (k_rows, tile), 1)

    def multiply(d):
        owner = lax.rem(z + (n_tm - d), n_tm)
        place = lax.rem(owner, per_tile)
        held = (lane >= place * cols) & (lane < (place + 1) * cols)
        columns = pl.ds(pl.multiple_of(owner // per_tile * tile, tile), tile)

        def one(o, carry):
            right = [
                jnp.concatenate([w[d, o, block] for block in range(n_space)], axis=1) for w in (w_h, w_l)
            ]
            m = dot3(elem_h[o], elem_l[o], *right, contract=1)
            real = m[:k_rows, :lanes] - m[k_rows:, lanes:]
            imag = m[:k_rows, lanes:] + m[k_rows:, :lanes]
            for reim, value in ((0, real), (1, imag)):
                if lanes < tile:
                    value = jnp.concatenate([value, jnp.zeros((k_rows, tile - lanes), f32)], axis=1)
                for a in range(nb):
                    moved = pltpu.roll(value, lax.rem(place * cols + (tile - a * cols), tile), 1)
                    out_ref[reim, o, 0, a, :, columns] = jnp.where(
                        held, moved, out_ref[reim, o, 0, a, :, columns]
                    )
            return carry

        lax.fori_loop(0, n_op, one, 0)

    multiply(0)
    before = None
    for d in order + [None]:
        if d is not None:
            take_x(d)
        if before is not None:
            for e in range(1, n_space):
                from_sibling[e, before].wait_recv()
                mix(e, before)
            multiply(before)
        before = d

    for copy in sent:
        copy.wait_send()


def local(n_tm, n_space, n_spin, eigenvectors, displaced, perambulators, gamma_values, spin_pattern, directions, momenta):
    _, _, colours, sites, width = eigenvectors.shape
    n_dir = displaced.shape[1]
    n_op = gamma_values.shape[1]
    perambulators = jnp.swapaxes(perambulators, 3, 4)
    _, _, nb, cols, l_rows = perambulators.shape
    rows = width // (n_space * n_spin)
    k_rows = width // n_space
    lanes = nb * cols
    depth = 2 * colours * sites
    operands = (eigenvectors, displaced, perambulators, gamma_values, spin_pattern, directions, momenta)
    dma = pltpu.SemaphoreType.DMA
    smem = pltpu.SMEM
    hbm = pl.BlockSpec(memory_space=pltpu.HBM)
    return pl.pallas_call(
        functools.partial(exchange, n_tm, n_space, n_spin),
        out_shape=pltpu.VMEM((2, n_op, 1, nb, k_rows, n_tm * cols), f32),
        in_specs=[hbm] * 7,
        out_specs=pl.BlockSpec(memory_space=pltpu.VMEM),
        scratch_shapes=[
            smem(gamma_values.shape, f32),
            smem(spin_pattern.shape, jnp.int32),
            smem(directions.shape, jnp.int32),
            smem(momenta.shape, jnp.int32),
            pltpu.VMEM((2, colours, sites, width), f32),
            pltpu.VMEM((n_dir, 2, colours, sites, width), f32),
            pltpu.VMEM((2 * width, depth), bf16),
            pltpu.VMEM((2 * width, depth), bf16),
            pltpu.VMEM((n_dir, n_spin, n_space, 2, rows, width), f32),
            pltpu.VMEM((n_dir, n_space, 2, rows, width), f32),
            pltpu.VMEM((n_dir, n_space, 2, rows, width), f32),
            pltpu.VMEM((n_dir, n_space, 2, rows, width), f32),
            pltpu.VMEM((n_space, n_tm, n_spin, 2, nb, cols, l_rows), f32),
            pltpu.VMEM((n_spin, n_op, 2, rows, width), f32),
            pltpu.VMEM((n_op, 2 * k_rows, width), bf16),
            pltpu.VMEM((n_op, 2 * k_rows, width), bf16),
            pltpu.VMEM((n_tm, n_op, n_space, 2 * lanes, l_rows), bf16),
            pltpu.VMEM((n_tm, n_op, n_space, 2 * lanes, l_rows), bf16),
            dma((6 + n_dir,)),
            dma((n_tm,)), dma((n_tm,)),
            dma((n_space, n_tm)), dma((n_space, n_tm)),
            dma((n_space, n_tm)), dma((n_space, n_tm)),
            dma((n_dir,)), dma((n_dir,)),
            dma((n_dir, n_space)), dma((n_dir, n_space)),
            dma((1,)), dma((1,)),
        ],
        compiler_params=pltpu.CompilerParams(
            collective_id=0, has_side_effects=True, vmem_limit_bytes=48 * 2**20
        ),
        name="exchange_and_multiply",
    )(*[pltpu.with_memory_space_constraint(v, pltpu.HBM) for v in operands])


def solution(mesh):
    in_specs = (
        P(None, ("parts", "tm"), None, ("space", "spin"), None),
        P(None, None, ("parts", "tm"), None, ("space", "spin"), None),
        P(None, "parts", "spin", "space", "tm"),
        P(),
        P(),
        P(),
        P(),
    )
    out_specs = P(None, None, ("parts", "tm"), "spin", "space", None)
    run = functools.partial(local, mesh.shape["tm"], mesh.shape["space"], mesh.shape["spin"])
    return jax.shard_map(run, mesh=mesh, in_specs=in_specs, out_specs=out_specs, check_vma=False)
```

```python
import functools
import math

import jax
import jax.numpy as jnp
import numpy as np
from jax import lax
from jax.experimental import pallas as pl
from jax.experimental.pallas import tpu as pltpu
from jax.sharding import PartitionSpec as P

MESH = pl.DeviceIdType.MESH
f32 = jnp.float32
bf16 = jnp.bfloat16


def split(value):
    high = value.astype(bf16)
    return high, (value - high.astype(f32)).astype(bf16)


def dot3(a_high, a_low, b_high, b_low, contract=0):
    dims = (((1,), (contract,)), ((), ()))
    dot = functools.partial(lax.dot_general, dimension_numbers=dims, preferred_element_type=f32)
    return dot(a_high, b_high) + (dot(a_high, b_low) + dot(a_low, b_high))


def table(index, values):
    result = f32(values[0])
    for j in range(1, len(values)):
        result = jnp.where(index == j, f32(values[j]), result)
    return result


def exchange(
    n_tm, n_space, n_spin,
    vec_hbm, dis_hbm, per_hbm, gamma_hbm, pattern_hbm, directions_hbm, momenta_hbm,
    out_ref,
    gamma, pattern, directions, momenta,
    vec, dis, lhs_h, lhs_l, part, part_in, g_out, g_in,
    slots, elem, elem_h, elem_l, w_h, w_l,
    load_sem, z_send, z_recv, x_send, x_recv, s_send, s_recv,
    gs_send, gs_recv, gx_send, gx_recv, e_send, e_recv,
):
    n_op = gamma.shape[1]
    n_dir = dis_hbm.shape[1]
    nb = per_hbm.shape[2]
    rows = part.shape[4]
    width = part.shape[5]
    cols = per_hbm.shape[3]
    lanes = nb * cols
    z = lax.axis_index("tm")
    x = lax.axis_index("space")
    c = lax.axis_index("spin")
    other = 1 - c

    def tm_peer(d):
        return {"tm": lax.rem(z + d, n_tm)}

    def x_peer(e):
        return {"space": lax.rem(x + e, n_space)}

    sibling = {"spin": other}

    own = pltpu.make_async_copy(per_hbm.at[:, z], slots.at[0, 0, c], load_sem.at[0])
    loads = [pltpu.make_async_copy(vec_hbm.at[:, 0], vec, load_sem.at[1])]
    for k in range(n_dir):
        loads.append(pltpu.make_async_copy(dis_hbm.at[:, k, 0], dis.at[k], load_sem.at[2 + k]))
    small = [(gamma_hbm, gamma), (pattern_hbm, pattern), (directions_hbm, directions), (momenta_hbm, momenta)]
    tables = [
        pltpu.make_async_copy(src, dst, load_sem.at[2 + n_dir + k]) for k, (src, dst) in enumerate(small)
    ]
    for load in loads + [own] + tables:
        load.start()

    order = sorted(range(1, n_tm), key=lambda d: min(d, n_tm - d))
    straight = order[:1]

    def both_peer(e, d):
        return {**tm_peer(d), **x_peer(e)}

    peers = [both_peer(n_space - e, n_tm - d) for d in straight for e in range(1, n_space)]
    peers += [tm_peer(d) for d in range(1, n_tm)] + [x_peer(e) for e in range(1, n_space)] + [sibling]
    barrier = pltpu.get_barrier_semaphore()
    for peer in peers:
        pl.semaphore_signal(barrier, inc=1, device_id=peer, device_id_type=MESH)
    pl.semaphore_wait(barrier, len(peers))

    sent = []

    def send(src, dst, send_sem, recv_sem, peer):
        copy = pltpu.make_async_remote_copy(
            src_ref=src, dst_ref=dst, send_sem=send_sem, recv_sem=recv_sem,
            device_id=peer, device_id_type=MESH,
        )
        copy.start()
        sent.append(copy)
        return copy

    from_sibling = {}
    from_x = {}
    from_z = {}

    def forward_sibling(e, d, src=None):
        from_sibling[e, d] = send(
            slots.at[e, d, c] if src is None else src, slots.at[e, d, c], s_send.at[e, d], s_recv.at[e, d], sibling
        )

    def forward_x(d, src=None):
        for e in range(1, n_space):
            from_x[e, d] = send(
                slots.at[0, d, c] if src is None else src, slots.at[e, d, c], x_send.at[e, d], x_recv.at[e, d], x_peer(e)
            )

    forward_x(0, per_hbm.at[:, z])
    for d in order:
        from_z[d] = send(
            per_hbm.at[:, lax.rem(z + d, n_tm)], slots.at[0, d, c], z_send.at[d], z_recv.at[d], tm_peer(d)
        )
        if d in straight:
            for e in range(1, n_space):
                from_x[e, d] = send(
                    per_hbm.at[:, lax.rem(z + d, n_tm)], slots.at[e, d, c],
                    x_send.at[e, d], x_recv.at[e, d], both_peer(e, d),
                )
    forward_sibling(0, 0, per_hbm.at[:, z])

    depth = lhs_h.shape[1]
    half = depth // 2
    loads[0].wait()
    turned = vec[...].reshape(depth, width).T
    high, low = split(turned)
    for ref, value in ((lhs_h, high), (lhs_l, low)):
        ref[:width] = value
        ref[width:, :half] = -value[:, half:]
        ref[width:, half:] = value[:, :half]
    from_part = []
    to_x = {}

    def reduce_part(k):
        from_part[k].wait_recv()
        for e in range(n_space):
            dest = lax.rem(x + e, n_space)
            total = part[k, c, dest] + part_in[k, dest]
            if e == 0:
                g_in[k, 0] = total
            else:
                g_out[k, e] = total
                to_x[k, e] = send(
                    g_out.at[k, e], g_in.at[k, e], gx_send.at[k, e], gx_recv.at[k, e], x_peer(e)
                )

    def pass_on(d):
        from_z[d].wait_recv()
        if d not in straight:
            forward_x(d)
        forward_sibling(0, d)

    for k in range(n_dir):
        loads[1 + k].wait()
        r_high, r_low = split(dis[k].reshape(depth, width))
        sums = dot3(lhs_h[...], lhs_l[...], r_high, r_low)
        for xb in range(n_space):
            for cb in range(n_spin):
                first = (xb * n_spin + cb) * rows
                for reim in range(2):
                    start = reim * width + first
                    part[k, cb, xb, reim] = sums[start : start + rows]
        from_part.append(
            send(part.at[k, other], part_in.at[k], gs_send.at[k], gs_recv.at[k], sibling)
        )
        if k > 0:
            reduce_part(k - 1)
        if k == 1:
            pass_on(order[0])
    reduce_part(n_dir - 1)
    for d in order[1:]:
        pass_on(d)

    def mix_one(e, d, o):
        block = lax.rem(x + (n_space - e), n_space)
        for a in range(nb):
            q_re = q_im = None
            row = c * nb + a
            for cb in range(n_spin):
                for b in range(nb):
                    present = pattern[o, row, cb * nb + b].astype(f32)
                    s_re = gamma[0, o, row, cb * nb + b] * present
                    s_im = gamma[1, o, row, cb * nb + b] * present
                    real = slots[e, d, cb, 0, b]
                    imag = slots[e, d, cb, 1, b]
                    t_re = s_re * real - s_im * imag
                    t_im = s_re * imag + s_im * real
                    q_re = t_re if q_re is None else q_re + t_re
                    q_im = t_im if q_im is None else q_im + t_im
            for reim, value in ((0, q_re), (1, q_im)):
                high, low = split(value)
                first = reim * lanes + a * cols
                w_h[d, o, block, first : first + cols] = high
                w_l[d, o, block, first : first + cols] = low

    def mix(e, d):
        def one(o, carry):
            mix_one(e, d, o)
            return carry

        lax.fori_loop(0, n_op, one, 0)

    def take_x(d):
        for e in range(1, n_space):
            from_x[e, d].wait_recv()
            forward_sibling(e, d)

    for copy in tables + [own]:
        copy.wait()
    take_x(0)
    for d in [0] + order:
        from_sibling[0, d].wait_recv()
        mix(0, d)
    for e in range(1, n_space):
        from_sibling[e, 0].wait_recv()
        mix(e, 0)

    for copy in to_x.values():
        copy.wait_recv()
    angles = np.arange(n_space, dtype=np.float32) * np.float32(2.0 * math.pi / n_space)
    cosines = [float(v) for v in np.cos(angles)]
    sines = [float(v) for v in np.sin(angles)]
    for o in range(n_op):
        e_re = jnp.zeros((rows, width), f32)
        e_im = jnp.zeros((rows, width), f32)
        way = directions[o]
        for e in range(n_space):
            plane = lax.rem(x + (n_space - e), n_space)
            step = lax.rem(momenta[o] * plane, n_space)
            cos_s = table(step, cosines)
            sin_s = table(step, sines)
            g_re = g_in[way, e, 0]
            g_im = g_in[way, e, 1]
            e_re += cos_s * g_re + sin_s * g_im
            e_im += cos_s * g_im - sin_s * g_re
        elem[c, o, 0] = e_re
        elem[c, o, 1] = e_im
    elem_copy = send(elem.at[c], elem.at[c], e_send.at[0], e_recv.at[0], sibling)
    k_rows = n_spin * rows
    elem_copy.wait_recv()
    for o in range(n_op):
        for reim in range(2):
            value = jnp.concatenate([elem[cb, o, reim] for cb in range(n_spin)], axis=0)
            high, low = split(value)
            elem_h[o, reim * k_rows : (reim + 1) * k_rows] = high
            elem_l[o, reim * k_rows : (reim + 1) * k_rows] = low

    tile = 128
    per_tile = tile // cols
    lane = lax.broadcasted_iota(jnp.int32, (k_rows, tile), 1)

    def multiply(d, fresh=()):
        owner = lax.rem(z + (n_tm - d), n_tm)
        place = lax.rem(owner, per_tile)
        held = (lane >= place * cols) & (lane < (place + 1) * cols)
        columns = pl.ds(pl.multiple_of(owner // per_tile * tile, tile), tile)

        for o in range(n_op):
            for e in fresh:
                mix_one(e, d, o)
            right = [
                jnp.concatenate([w[d, o, block] for block in range(n_space)], axis=1) for w in (w_h, w_l)
            ]
            m = dot3(elem_h[o], elem_l[o], *right, contract=1)
            real = m[:k_rows, :lanes] - m[k_rows:, lanes:]
            imag = m[:k_rows, lanes:] + m[k_rows:, :lanes]
            for reim, value in ((0, real), (1, imag)):
                if lanes < tile:
                    value = jnp.concatenate([value, jnp.zeros((k_rows, tile - lanes), f32)], axis=1)
                for a in range(nb):
                    moved = pltpu.roll(value, lax.rem(place * cols + (tile - a * cols), tile), 1)
                    out_ref[reim, o, 0, a, :, columns] = jnp.where(
                        held, moved, out_ref[reim, o, 0, a, :, columns]
                    )

    multiply(0)
    before = None
    for d in order + [None]:
        if d is not None:
            take_x(d)
        if before is not None:
            for e in range(1, n_space):
                from_sibling[e, before].wait_recv()
            multiply(before, range(1, n_space))
        before = d

    for copy in sent:
        copy.wait_send()


def local(n_tm, n_space, n_spin, eigenvectors, displaced, perambulators, gamma_values, spin_pattern, directions, momenta):
    _, _, colours, sites, width = eigenvectors.shape
    n_dir = displaced.shape[1]
    n_op = gamma_values.shape[1]
    perambulators = jnp.swapaxes(perambulators, 3, 4)
    _, _, nb, cols, l_rows = perambulators.shape
    rows = width // (n_space * n_spin)
    k_rows = width // n_space
    lanes = nb * cols
    depth = 2 * colours * sites
    operands = (eigenvectors, displaced, perambulators, gamma_values, spin_pattern, directions, momenta)
    dma = pltpu.SemaphoreType.DMA
    smem = pltpu.SMEM
    hbm = pl.BlockSpec(memory_space=pltpu.HBM)
    return pl.pallas_call(
        functools.partial(exchange, n_tm, n_space, n_spin),
        out_shape=pltpu.VMEM((2, n_op, 1, nb, k_rows, n_tm * cols), f32),
        in_specs=[hbm] * 7,
        out_specs=pl.BlockSpec(memory_space=pltpu.VMEM),
        scratch_shapes=[
            smem(gamma_values.shape, f32),
            smem(spin_pattern.shape, jnp.int32),
            smem(directions.shape, jnp.int32),
            smem(momenta.shape, jnp.int32),
            pltpu.VMEM((2, colours, sites, width), f32),
            pltpu.VMEM((n_dir, 2, colours, sites, width), f32),
            pltpu.VMEM((2 * width, depth), bf16),
            pltpu.VMEM((2 * width, depth), bf16),
            pltpu.VMEM((n_dir, n_spin, n_space, 2, rows, width), f32),
            pltpu.VMEM((n_dir, n_space, 2, rows, width), f32),
            pltpu.VMEM((n_dir, n_space, 2, rows, width), f32),
            pltpu.VMEM((n_dir, n_space, 2, rows, width), f32),
            pltpu.VMEM((n_space, n_tm, n_spin, 2, nb, cols, l_rows), f32),
            pltpu.VMEM((n_spin, n_op, 2, rows, width), f32),
            pltpu.VMEM((n_op, 2 * k_rows, width), bf16),
            pltpu.VMEM((n_op, 2 * k_rows, width), bf16),
            pltpu.VMEM((n_tm, n_op, n_space, 2 * lanes, l_rows), bf16),
            pltpu.VMEM((n_tm, n_op, n_space, 2 * lanes, l_rows), bf16),
            dma((6 + n_dir,)),
            dma((n_tm,)), dma((n_tm,)),
            dma((n_space, n_tm)), dma((n_space, n_tm)),
            dma((n_space, n_tm)), dma((n_space, n_tm)),
            dma((n_dir,)), dma((n_dir,)),
            dma((n_dir, n_space)), dma((n_dir, n_space)),
            dma((1,)), dma((1,)),
        ],
        compiler_params=pltpu.CompilerParams(
            collective_id=0, has_side_effects=True, vmem_limit_bytes=48 * 2**20
        ),
        name="exchange_and_multiply",
    )(*[pltpu.with_memory_space_constraint(v, pltpu.HBM) for v in operands])


def solution(mesh):
    in_specs = (
        P(None, ("parts", "tm"), None, ("space", "spin"), None),
        P(None, None, ("parts", "tm"), None, ("space", "spin"), None),
        P(None, "parts", "spin", "space", "tm"),
        P(),
        P(),
        P(),
        P(),
    )
    out_specs = P(None, None, ("parts", "tm"), "spin", "space", None)
    run = functools.partial(local, mesh.shape["tm"], mesh.shape["space"], mesh.shape["spin"])
    return jax.shard_map(run, mesh=mesh, in_specs=in_specs, out_specs=out_specs, check_vma=False)
```

```python
import functools
import math

import jax
import jax.numpy as jnp
import numpy as np
from jax import lax
from jax.experimental import pallas as pl
from jax.experimental.pallas import tpu as pltpu
from jax.sharding import PartitionSpec as P

MESH = pl.DeviceIdType.MESH
f32 = jnp.float32
bf16 = jnp.bfloat16


def split(value):
    high = value.astype(bf16)
    return high, (value - high.astype(f32)).astype(bf16)


def dot3(a_high, a_low, b_high, b_low, contract=0):
    dims = (((1,), (contract,)), ((), ()))
    dot = functools.partial(lax.dot_general, dimension_numbers=dims, preferred_element_type=f32)
    return dot(a_high, b_high) + (dot(a_high, b_low) + dot(a_low, b_high))


def block_product(o, owner, elem_h, elem_l, rights, before, after):
    nb, k_rows = before.shape[3:5]
    lanes = rights[0].shape[2] // 2
    cols = lanes // nb
    tile = 128
    per_tile = tile // cols
    lane = lax.broadcasted_iota(jnp.int32, (k_rows, tile), 1)
    place = lax.rem(owner, per_tile)
    held = (lane >= place * cols) & (lane < (place + 1) * cols)
    columns = pl.ds(pl.multiple_of(owner // per_tile * tile, tile), tile)
    right = [jnp.concatenate([w[o, block] for block in range(w.shape[1])], axis=1) for w in rights]
    m = dot3(elem_h[o], elem_l[o], *right, contract=1)
    real = m[:k_rows, :lanes] - m[k_rows:, lanes:]
    imag = m[:k_rows, lanes:] + m[k_rows:, :lanes]
    for reim, value in ((0, real), (1, imag)):
        if lanes < tile:
            value = jnp.concatenate([value, jnp.zeros((k_rows, tile - lanes), f32)], axis=1)
        for a in range(nb):
            moved = pltpu.roll(value, lax.rem(place * cols + (tile - a * cols), tile), 1)
            after[reim, o, 0, a, :, columns] = jnp.where(held, moved, before[reim, o, 0, a, :, columns])


def table(index, values):
    result = f32(values[0])
    for j in range(1, len(values)):
        result = jnp.where(index == j, f32(values[j]), result)
    return result


def exchange(
    n_tm, n_space, n_spin,
    vec_hbm, dis_hbm, per_hbm, gamma_hbm, pattern_hbm, directions_hbm, momenta_hbm,
    out_ref, elem_h, elem_l, last_h, last_l,
    gamma, pattern, directions, momenta,
    vec, dis, lhs_h, lhs_l, part, part_in, g_out, g_in,
    slots, elem, w_h, w_l,
    load_sem, z_send, z_recv, x_send, x_recv, s_send, s_recv,
    gs_send, gs_recv, gx_send, gx_recv, e_send, e_recv,
):
    n_op = gamma.shape[1]
    n_dir = dis_hbm.shape[1]
    nb = per_hbm.shape[2]
    rows = part.shape[4]
    width = part.shape[5]
    cols = per_hbm.shape[3]
    lanes = nb * cols
    z = lax.axis_index("tm")
    x = lax.axis_index("space")
    c = lax.axis_index("spin")
    other = 1 - c

    def tm_peer(d):
        return {"tm": lax.rem(z + d, n_tm)}

    def x_peer(e):
        return {"space": lax.rem(x + e, n_space)}

    sibling = {"spin": other}

    own = pltpu.make_async_copy(per_hbm.at[:, z], slots.at[0, 0, c], load_sem.at[0])
    loads = [pltpu.make_async_copy(vec_hbm.at[:, 0], vec, load_sem.at[1])]
    for k in range(n_dir):
        loads.append(pltpu.make_async_copy(dis_hbm.at[:, k, 0], dis.at[k], load_sem.at[2 + k]))
    small = [(gamma_hbm, gamma), (pattern_hbm, pattern), (directions_hbm, directions), (momenta_hbm, momenta)]
    tables = [
        pltpu.make_async_copy(src, dst, load_sem.at[2 + n_dir + k]) for k, (src, dst) in enumerate(small)
    ]
    for load in loads + [own] + tables:
        load.start()

    order = sorted(range(1, n_tm), key=lambda d: min(d, n_tm - d))
    straight = order[:1]

    def both_peer(e, d):
        return {**tm_peer(d), **x_peer(e)}

    peers = [both_peer(n_space - e, n_tm - d) for d in straight for e in range(1, n_space)]
    peers += [tm_peer(d) for d in range(1, n_tm)] + [x_peer(e) for e in range(1, n_space)] + [sibling]
    barrier = pltpu.get_barrier_semaphore()
    for peer in peers:
        pl.semaphore_signal(barrier, inc=1, device_id=peer, device_id_type=MESH)
    pl.semaphore_wait(barrier, len(peers))

    sent = []

    def send(src, dst, send_sem, recv_sem, peer):
        copy = pltpu.make_async_remote_copy(
            src_ref=src, dst_ref=dst, send_sem=send_sem, recv_sem=recv_sem,
            device_id=peer, device_id_type=MESH,
        )
        copy.start()
        sent.append(copy)
        return copy

    from_sibling = {}
    from_x = {}
    from_z = {}

    def forward_sibling(e, d, src=None):
        from_sibling[e, d] = send(
            slots.at[e, d, c] if src is None else src, slots.at[e, d, c], s_send.at[e, d], s_recv.at[e, d], sibling
        )

    def forward_x(d, src=None):
        for e in range(1, n_space):
            from_x[e, d] = send(
                slots.at[0, d, c] if src is None else src, slots.at[e, d, c], x_send.at[e, d], x_recv.at[e, d], x_peer(e)
            )

    forward_x(0, per_hbm.at[:, z])
    for d in order:
        from_z[d] = send(
            per_hbm.at[:, lax.rem(z + d, n_tm)], slots.at[0, d, c], z_send.at[d], z_recv.at[d], tm_peer(d)
        )
        if d in straight:
            for e in range(1, n_space):
                from_x[e, d] = send(
                    per_hbm.at[:, lax.rem(z + d, n_tm)], slots.at[e, d, c],
                    x_send.at[e, d], x_recv.at[e, d], both_peer(e, d),
                )
    forward_sibling(0, 0, per_hbm.at[:, z])

    depth = lhs_h.shape[1]
    half = depth // 2
    loads[0].wait()
    turned = vec[...].reshape(depth, width).T
    high, low = split(turned)
    for ref, value in ((lhs_h, high), (lhs_l, low)):
        ref[:width] = value
        ref[width:, :half] = -value[:, half:]
        ref[width:, half:] = value[:, :half]
    from_part = []
    to_x = {}

    def reduce_part(k):
        from_part[k].wait_recv()
        for e in range(n_space):
            dest = lax.rem(x + e, n_space)
            total = part[k, c, dest] + part_in[k, dest]
            if e == 0:
                g_in[k, 0] = total
            else:
                g_out[k, e] = total
                to_x[k, e] = send(
                    g_out.at[k, e], g_in.at[k, e], gx_send.at[k, e], gx_recv.at[k, e], x_peer(e)
                )

    def pass_on(d):
        from_z[d].wait_recv()
        if d not in straight:
            forward_x(d)
        forward_sibling(0, d)

    for k in range(n_dir):
        loads[1 + k].wait()
        r_high, r_low = split(dis[k].reshape(depth, width))
        sums = dot3(lhs_h[...], lhs_l[...], r_high, r_low)
        for xb in range(n_space):
            for cb in range(n_spin):
                first = (xb * n_spin + cb) * rows
                for reim in range(2):
                    start = reim * width + first
                    part[k, cb, xb, reim] = sums[start : start + rows]
        from_part.append(
            send(part.at[k, other], part_in.at[k], gs_send.at[k], gs_recv.at[k], sibling)
        )
        if k > 0:
            reduce_part(k - 1)
        if k == 1:
            pass_on(order[0])
    reduce_part(n_dir - 1)
    for d in order[1:]:
        pass_on(d)

    def mix_one(e, d, o, to_h=None, to_l=None):
        to_h = w_h.at[d] if to_h is None else to_h
        to_l = w_l.at[d] if to_l is None else to_l
        block = lax.rem(x + (n_space - e), n_space)
        for a in range(nb):
            q_re = q_im = None
            row = c * nb + a
            for cb in range(n_spin):
                for b in range(nb):
                    present = pattern[o, row, cb * nb + b].astype(f32)
                    s_re = gamma[0, o, row, cb * nb + b] * present
                    s_im = gamma[1, o, row, cb * nb + b] * present
                    real = slots[e, d, cb, 0, b]
                    imag = slots[e, d, cb, 1, b]
                    t_re = s_re * real - s_im * imag
                    t_im = s_re * imag + s_im * real
                    q_re = t_re if q_re is None else q_re + t_re
                    q_im = t_im if q_im is None else q_im + t_im
            for reim, value in ((0, q_re), (1, q_im)):
                high, low = split(value)
                first = reim * lanes + a * cols
                to_h[o, block, first : first + cols] = high
                to_l[o, block, first : first + cols] = low

    def mix(e, d):
        def one(o, carry):
            mix_one(e, d, o, *((last_h, last_l) if d == order[-1] else ()))
            return carry

        lax.fori_loop(0, n_op, one, 0)

    def take_x(d):
        for e in range(1, n_space):
            from_x[e, d].wait_recv()
            forward_sibling(e, d)

    for copy in tables + [own]:
        copy.wait()
    take_x(0)
    for d in [0] + order:
        from_sibling[0, d].wait_recv()
        mix(0, d)
    for e in range(1, n_space):
        from_sibling[e, 0].wait_recv()
        mix(e, 0)

    for copy in to_x.values():
        copy.wait_recv()
    angles = np.arange(n_space, dtype=np.float32) * np.float32(2.0 * math.pi / n_space)
    cosines = [float(v) for v in np.cos(angles)]
    sines = [float(v) for v in np.sin(angles)]
    for o in range(n_op):
        e_re = jnp.zeros((rows, width), f32)
        e_im = jnp.zeros((rows, width), f32)
        way = directions[o]
        for e in range(n_space):
            plane = lax.rem(x + (n_space - e), n_space)
            step = lax.rem(momenta[o] * plane, n_space)
            cos_s = table(step, cosines)
            sin_s = table(step, sines)
            g_re = g_in[way, e, 0]
            g_im = g_in[way, e, 1]
            e_re += cos_s * g_re + sin_s * g_im
            e_im += cos_s * g_im - sin_s * g_re
        elem[c, o, 0] = e_re
        elem[c, o, 1] = e_im
    elem_copy = send(elem.at[c], elem.at[c], e_send.at[0], e_recv.at[0], sibling)
    k_rows = n_spin * rows
    elem_copy.wait_recv()
    for o in range(n_op):
        for reim in range(2):
            value = jnp.concatenate([elem[cb, o, reim] for cb in range(n_spin)], axis=0)
            high, low = split(value)
            elem_h[o, reim * k_rows : (reim + 1) * k_rows] = high
            elem_l[o, reim * k_rows : (reim + 1) * k_rows] = low

    def multiply(d, unroll):
        owner = lax.rem(z + (n_tm - d), n_tm)

        def one(o, carry):
            for e in range(1, n_space):
                if d > 0:
                    mix_one(e, d, o)
            block_product(o, owner, elem_h, elem_l, (w_h.at[d], w_l.at[d]), out_ref, out_ref)
            return carry

        if unroll:
            for o in range(n_op):
                one(o, 0)
        else:
            lax.fori_loop(0, n_op, one, 0)

    multiply(0, False)
    before = None
    for d in order:
        take_x(d)
        if before is not None:
            for e in range(1, n_space):
                from_sibling[e, before].wait_recv()
            multiply(before, d == order[-1])
        before = d
    for e in range(1, n_space):
        from_sibling[e, before].wait_recv()
        for o in range(n_op):
            mix_one(e, before, o, last_h, last_l)
    for copy in sent:
        copy.wait_send()


def finish(n_tm, y_ref, elem_h, elem_l, last_h, last_l, out_hbm, whole, out_sem):
    order = sorted(range(1, n_tm), key=lambda d: min(d, n_tm - d))
    owner = lax.rem(lax.axis_index("tm") + (n_tm - order[-1]), n_tm)
    copies = []
    for o in range(y_ref.shape[1]):
        whole[:, o] = y_ref[:, o]
        block_product(o, owner, elem_h, elem_l, (last_h, last_l), y_ref, whole)
        copies.append(pltpu.make_async_copy(whole.at[:, o], out_hbm.at[:, o], out_sem.at[o]))
        copies[-1].start()
    for copy in copies:
        copy.wait()


def local(n_tm, n_space, n_spin, eigenvectors, displaced, perambulators, gamma_values, spin_pattern, directions, momenta):
    _, _, colours, sites, width = eigenvectors.shape
    n_dir = displaced.shape[1]
    n_op = gamma_values.shape[1]
    perambulators = jnp.swapaxes(perambulators, 3, 4)
    _, _, nb, cols, l_rows = perambulators.shape
    rows = width // (n_space * n_spin)
    k_rows = width // n_space
    lanes = nb * cols
    depth = 2 * colours * sites
    operands = (eigenvectors, displaced, perambulators, gamma_values, spin_pattern, directions, momenta)
    out_dims = (2, n_op, 1, nb, k_rows, n_tm * cols)
    dma = pltpu.SemaphoreType.DMA
    smem = pltpu.SMEM
    hbm = pl.BlockSpec(memory_space=pltpu.HBM)
    y, *factors = pl.pallas_call(
        functools.partial(exchange, n_tm, n_space, n_spin),
        out_shape=[
            pltpu.VMEM(out_dims, f32),
            pltpu.VMEM((n_op, 2 * k_rows, width), bf16),
            pltpu.VMEM((n_op, 2 * k_rows, width), bf16),
            pltpu.VMEM((n_op, n_space, 2 * lanes, l_rows), bf16),
            pltpu.VMEM((n_op, n_space, 2 * lanes, l_rows), bf16),
        ],
        in_specs=[hbm] * 7,
        out_specs=[pl.BlockSpec(memory_space=pltpu.VMEM)] * 5,
        scratch_shapes=[
            smem(gamma_values.shape, f32),
            smem(spin_pattern.shape, jnp.int32),
            smem(directions.shape, jnp.int32),
            smem(momenta.shape, jnp.int32),
            pltpu.VMEM((2, colours, sites, width), f32),
            pltpu.VMEM((n_dir, 2, colours, sites, width), f32),
            pltpu.VMEM((2 * width, depth), bf16),
            pltpu.VMEM((2 * width, depth), bf16),
            pltpu.VMEM((n_dir, n_spin, n_space, 2, rows, width), f32),
            pltpu.VMEM((n_dir, n_space, 2, rows, width), f32),
            pltpu.VMEM((n_dir, n_space, 2, rows, width), f32),
            pltpu.VMEM((n_dir, n_space, 2, rows, width), f32),
            pltpu.VMEM((n_space, n_tm, n_spin, 2, nb, cols, l_rows), f32),
            pltpu.VMEM((n_spin, n_op, 2, rows, width), f32),
            pltpu.VMEM((n_tm, n_op, n_space, 2 * lanes, l_rows), bf16),
            pltpu.VMEM((n_tm, n_op, n_space, 2 * lanes, l_rows), bf16),
            dma((6 + n_dir,)),
            dma((n_tm,)), dma((n_tm,)),
            dma((n_space, n_tm)), dma((n_space, n_tm)),
            dma((n_space, n_tm)), dma((n_space, n_tm)),
            dma((n_dir,)), dma((n_dir,)),
            dma((n_dir, n_space)), dma((n_dir, n_space)),
            dma((1,)), dma((1,)),
        ],
        compiler_params=pltpu.CompilerParams(
            collective_id=0, has_side_effects=True, vmem_limit_bytes=48 * 2**20
        ),
        name="exchange_and_multiply",
    )(*[pltpu.with_memory_space_constraint(v, pltpu.HBM) for v in operands])
    return pl.pallas_call(
        functools.partial(finish, n_tm),
        out_shape=jax.ShapeDtypeStruct(out_dims, f32),
        in_specs=[pl.BlockSpec(memory_space=pltpu.VMEM)] * 5,
        out_specs=pl.BlockSpec(memory_space=pltpu.HBM),
        scratch_shapes=[pltpu.VMEM(out_dims, f32), dma((n_op,))],
        compiler_params=pltpu.CompilerParams(vmem_limit_bytes=32 * 2**20),
        name="last_block",
    )(y, *factors)


def solution(mesh):
    in_specs = (
        P(None, ("parts", "tm"), None, ("space", "spin"), None),
        P(None, None, ("parts", "tm"), None, ("space", "spin"), None),
        P(None, "parts", "spin", "space", "tm"),
        P(),
        P(),
        P(),
        P(),
    )
    out_specs = P(None, None, ("parts", "tm"), "spin", "space", None)
    run = functools.partial(local, mesh.shape["tm"], mesh.shape["space"], mesh.shape["spin"])
    return jax.shard_map(run, mesh=mesh, in_specs=in_specs, out_specs=out_specs, check_vma=False)
```

```python
import functools
import math

import jax
import jax.numpy as jnp
import numpy as np
from jax import lax
from jax.experimental import pallas as pl
from jax.experimental.pallas import tpu as pltpu
from jax.sharding import PartitionSpec as P

MESH = pl.DeviceIdType.MESH
f32 = jnp.float32
bf16 = jnp.bfloat16


def split(value):
    high = value.astype(bf16)
    return high, (value - high.astype(f32)).astype(bf16)


def dot3(a_high, a_low, b_high, b_low, contract=0):
    dims = (((1,), (contract,)), ((), ()))
    dot = functools.partial(lax.dot_general, dimension_numbers=dims, preferred_element_type=f32)
    return dot(a_high, b_high) + (dot(a_high, b_low) + dot(a_low, b_high))


def table(index, values):
    result = f32(values[0])
    for j in range(1, len(values)):
        result = jnp.where(index == j, f32(values[j]), result)
    return result


def exchange(
    n_tm, n_space, n_spin,
    vec_hbm, dis_hbm, per_hbm, gamma_hbm, pattern_hbm, directions_hbm, momenta_hbm,
    out_ref,
    gamma, pattern, directions, momenta,
    vec, dis, lhs_h, lhs_l, part, part_in, g_out, g_in,
    slots, elem, elem_h, elem_l, w_h, w_l,
    load_sem, z_send, z_recv, x_send, x_recv, s_send, s_recv,
    gs_send, gs_recv, gx_send, gx_recv, e_send, e_recv,
):
    n_op = gamma.shape[1]
    n_dir = dis_hbm.shape[1]
    nb = per_hbm.shape[2]
    rows = part.shape[4]
    width = part.shape[5]
    cols = per_hbm.shape[3]
    lanes = nb * cols
    z = lax.axis_index("tm")
    x = lax.axis_index("space")
    c = lax.axis_index("spin")
    other = 1 - c

    def tm_peer(d):
        return {"tm": lax.rem(z + d, n_tm)}

    def x_peer(e):
        return {"space": lax.rem(x + e, n_space)}

    sibling = {"spin": other}

    own = pltpu.make_async_copy(per_hbm.at[:, z], slots.at[0, 0, c], load_sem.at[0])
    loads = [pltpu.make_async_copy(vec_hbm.at[:, 0], vec, load_sem.at[1])]
    for k in range(n_dir):
        loads.append(pltpu.make_async_copy(dis_hbm.at[:, k, 0], dis.at[k], load_sem.at[2 + k]))
    small = [(gamma_hbm, gamma), (pattern_hbm, pattern), (directions_hbm, directions), (momenta_hbm, momenta)]
    tables = [
        pltpu.make_async_copy(src, dst, load_sem.at[2 + n_dir + k]) for k, (src, dst) in enumerate(small)
    ]
    for load in loads + [own] + tables:
        load.start()

    order = sorted(range(1, n_tm), key=lambda d: min(d, n_tm - d))
    straight = order[:1]

    def both_peer(e, d):
        return {**tm_peer(d), **x_peer(e)}

    peers = [both_peer(n_space - e, n_tm - d) for d in straight for e in range(1, n_space)]
    peers += [tm_peer(d) for d in range(1, n_tm)] + [x_peer(e) for e in range(1, n_space)] + [sibling]
    barrier = pltpu.get_barrier_semaphore()
    for peer in peers:
        pl.semaphore_signal(barrier, inc=1, device_id=peer, device_id_type=MESH)
    pl.semaphore_wait(barrier, len(peers))

    sent = []

    def send(src, dst, send_sem, recv_sem, peer):
        copy = pltpu.make_async_remote_copy(
            src_ref=src, dst_ref=dst, send_sem=send_sem, recv_sem=recv_sem,
            device_id=peer, device_id_type=MESH,
        )
        copy.start()
        sent.append(copy)
        return copy

    from_sibling = {}
    from_x = {}
    from_z = {}

    def forward_sibling(e, d, src=None):
        from_sibling[e, d] = send(
            slots.at[e, d, c] if src is None else src, slots.at[e, d, c], s_send.at[e, d], s_recv.at[e, d], sibling
        )

    def forward_x(d, src=None):
        for e in range(1, n_space):
            from_x[e, d] = send(
                slots.at[0, d, c] if src is None else src, slots.at[e, d, c], x_send.at[e, d], x_recv.at[e, d], x_peer(e)
            )

    forward_x(0, per_hbm.at[:, z])
    for d in order:
        from_z[d] = send(
            per_hbm.at[:, lax.rem(z + d, n_tm)], slots.at[0, d, c], z_send.at[d], z_recv.at[d], tm_peer(d)
        )
        if d in straight:
            for e in range(1, n_space):
                from_x[e, d] = send(
                    per_hbm.at[:, lax.rem(z + d, n_tm)], slots.at[e, d, c],
                    x_send.at[e, d], x_recv.at[e, d], both_peer(e, d),
                )
    forward_sibling(0, 0, per_hbm.at[:, z])

    depth = lhs_h.shape[1]
    half = depth // 2
    loads[0].wait()
    turned = vec[...].reshape(depth, width).T
    high, low = split(turned)
    for ref, value in ((lhs_h, high), (lhs_l, low)):
        ref[:width] = value
        ref[width:, :half] = -value[:, half:]
        ref[width:, half:] = value[:, :half]
    from_part = []
    to_x = {}

    def reduce_part(k):
        from_part[k].wait_recv()
        for e in range(n_space):
            dest = lax.rem(x + e, n_space)
            total = part[k, c, dest] + part_in[k, dest]
            if e == 0:
                g_in[k, 0] = total
            else:
                g_out[k, e] = total
                to_x[k, e] = send(
                    g_out.at[k, e], g_in.at[k, e], gx_send.at[k, e], gx_recv.at[k, e], x_peer(e)
                )

    def pass_on(d):
        from_z[d].wait_recv()
        if d not in straight:
            forward_x(d)
        forward_sibling(0, d)

    for k in range(n_dir):
        loads[1 + k].wait()
        r_high, r_low = split(dis[k].reshape(depth, width))
        sums = dot3(lhs_h[...], lhs_l[...], r_high, r_low)
        for xb in range(n_space):
            for cb in range(n_spin):
                first = (xb * n_spin + cb) * rows
                for reim in range(2):
                    start = reim * width + first
                    part[k, cb, xb, reim] = sums[start : start + rows]
        from_part.append(
            send(part.at[k, other], part_in.at[k], gs_send.at[k], gs_recv.at[k], sibling)
        )
        if k > 0:
            reduce_part(k - 1)
        if k == 1:
            pass_on(order[0])
    reduce_part(n_dir - 1)
    for d in order[1:]:
        pass_on(d)

    def mix_one(e, d, o):
        block = lax.rem(x + (n_space - e), n_space)
        for a in range(nb):
            q_re = q_im = None
            row = c * nb + a
            for cb in range(n_spin):
                for b in range(nb):
                    present = pattern[o, row, cb * nb + b].astype(f32)
                    s_re = gamma[0, o, row, cb * nb + b] * present
                    s_im = gamma[1, o, row, cb * nb + b] * present
                    real = slots[e, d, cb, 0, b]
                    imag = slots[e, d, cb, 1, b]
                    t_re = s_re * real - s_im * imag
                    t_im = s_re * imag + s_im * real
                    q_re = t_re if q_re is None else q_re + t_re
                    q_im = t_im if q_im is None else q_im + t_im
            for reim, value in ((0, q_re), (1, q_im)):
                high, low = split(value)
                first = reim * lanes + a * cols
                w_h[d, o, block, first : first + cols] = high
                w_l[d, o, block, first : first + cols] = low

    def mix(e, d):
        def one(o, carry):
            mix_one(e, d, o)
            return carry

        lax.fori_loop(0, n_op, one, 0)

    def take_x(d):
        for e in range(1, n_space):
            from_x[e, d].wait_recv()
            forward_sibling(e, d)

    for copy in tables + [own]:
        copy.wait()
    take_x(0)
    for d in [0] + straight:
        from_sibling[0, d].wait_recv()
        mix(0, d)

    for copy in to_x.values():
        copy.wait_recv()
    angles = np.arange(n_space, dtype=np.float32) * np.float32(2.0 * math.pi / n_space)
    cosines = [float(v) for v in np.cos(angles)]
    sines = [float(v) for v in np.sin(angles)]
    for o in range(n_op):
        e_re = jnp.zeros((rows, width), f32)
        e_im = jnp.zeros((rows, width), f32)
        way = directions[o]
        for e in range(n_space):
            plane = lax.rem(x + (n_space - e), n_space)
            step = lax.rem(momenta[o] * plane, n_space)
            cos_s = table(step, cosines)
            sin_s = table(step, sines)
            g_re = g_in[way, e, 0]
            g_im = g_in[way, e, 1]
            e_re += cos_s * g_re + sin_s * g_im
            e_im += cos_s * g_im - sin_s * g_re
        elem[c, o, 0] = e_re
        elem[c, o, 1] = e_im
    elem_copy = send(elem.at[c], elem.at[c], e_send.at[0], e_recv.at[0], sibling)
    k_rows = n_spin * rows
    for e in range(1, n_space):
        from_sibling[e, 0].wait_recv()
        mix(e, 0)
    for d in order[1:]:
        from_sibling[0, d].wait_recv()
        mix(0, d)
    elem_copy.wait_recv()
    for o in range(n_op):
        for reim in range(2):
            value = jnp.concatenate([elem[cb, o, reim] for cb in range(n_spin)], axis=0)
            high, low = split(value)
            elem_h[o, reim * k_rows : (reim + 1) * k_rows] = high
            elem_l[o, reim * k_rows : (reim + 1) * k_rows] = low

    tile = 128
    per_tile = tile // cols
    lane = lax.broadcasted_iota(jnp.int32, (k_rows, tile), 1)

    def multiply(d, fresh=()):
        owner = lax.rem(z + (n_tm - d), n_tm)
        place = lax.rem(owner, per_tile)
        held = (lane >= place * cols) & (lane < (place + 1) * cols)
        columns = pl.ds(pl.multiple_of(owner // per_tile * tile, tile), tile)

        def one(o, carry):
            for e in fresh:
                mix_one(e, d, o)
            right = [
                jnp.concatenate([w[d, o, block] for block in range(n_space)], axis=1) for w in (w_h, w_l)
            ]
            m = dot3(elem_h[o], elem_l[o], *right, contract=1)
            real = m[:k_rows, :lanes] - m[k_rows:, lanes:]
            imag = m[:k_rows, lanes:] + m[k_rows:, :lanes]
            for reim, value in ((0, real), (1, imag)):
                if lanes < tile:
                    value = jnp.concatenate([value, jnp.zeros((k_rows, tile - lanes), f32)], axis=1)
                for a in range(nb):
                    moved = pltpu.roll(value, lax.rem(place * cols + (tile - a * cols), tile), 1)
                    out_ref[reim, o, 0, a, :, columns] = jnp.where(
                        held, moved, out_ref[reim, o, 0, a, :, columns]
                    )
            return carry

        if d in (0, order[0], *order[-2:]):
            for o in range(n_op):
                one(o, 0)
        else:
            lax.fori_loop(0, n_op, one, 0)

    multiply(0)
    before = None
    for d in order + [None]:
        if d is not None:
            take_x(d)
        if before is not None:
            for e in range(1, n_space):
                from_sibling[e, before].wait_recv()
            multiply(before, range(1, n_space))
        before = d

    for copy in sent:
        copy.wait_send()


def local(n_tm, n_space, n_spin, eigenvectors, displaced, perambulators, gamma_values, spin_pattern, directions, momenta):
    _, _, colours, sites, width = eigenvectors.shape
    n_dir = displaced.shape[1]
    n_op = gamma_values.shape[1]
    perambulators = jnp.swapaxes(perambulators, 3, 4)
    _, _, nb, cols, l_rows = perambulators.shape
    rows = width // (n_space * n_spin)
    k_rows = width // n_space
    lanes = nb * cols
    depth = 2 * colours * sites
    operands = (eigenvectors, displaced, perambulators, gamma_values, spin_pattern, directions, momenta)
    dma = pltpu.SemaphoreType.DMA
    smem = pltpu.SMEM
    hbm = pl.BlockSpec(memory_space=pltpu.HBM)
    return pl.pallas_call(
        functools.partial(exchange, n_tm, n_space, n_spin),
        out_shape=pltpu.VMEM((2, n_op, 1, nb, k_rows, n_tm * cols), f32),
        in_specs=[hbm] * 7,
        out_specs=pl.BlockSpec(memory_space=pltpu.VMEM),
        scratch_shapes=[
            smem(gamma_values.shape, f32),
            smem(spin_pattern.shape, jnp.int32),
            smem(directions.shape, jnp.int32),
            smem(momenta.shape, jnp.int32),
            pltpu.VMEM((2, colours, sites, width), f32),
            pltpu.VMEM((n_dir, 2, colours, sites, width), f32),
            pltpu.VMEM((2 * width, depth), bf16),
            pltpu.VMEM((2 * width, depth), bf16),
            pltpu.VMEM((n_dir, n_spin, n_space, 2, rows, width), f32),
            pltpu.VMEM((n_dir, n_space, 2, rows, width), f32),
            pltpu.VMEM((n_dir, n_space, 2, rows, width), f32),
            pltpu.VMEM((n_dir, n_space, 2, rows, width), f32),
            pltpu.VMEM((n_space, n_tm, n_spin, 2, nb, cols, l_rows), f32),
            pltpu.VMEM((n_spin, n_op, 2, rows, width), f32),
            pltpu.VMEM((n_op, 2 * k_rows, width), bf16),
            pltpu.VMEM((n_op, 2 * k_rows, width), bf16),
            pltpu.VMEM((n_tm, n_op, n_space, 2 * lanes, l_rows), bf16),
            pltpu.VMEM((n_tm, n_op, n_space, 2 * lanes, l_rows), bf16),
            dma((6 + n_dir,)),
            dma((n_tm,)), dma((n_tm,)),
            dma((n_space, n_tm)), dma((n_space, n_tm)),
            dma((n_space, n_tm)), dma((n_space, n_tm)),
            dma((n_dir,)), dma((n_dir,)),
            dma((n_dir, n_space)), dma((n_dir, n_space)),
            dma((1,)), dma((1,)),
        ],
        compiler_params=pltpu.CompilerParams(
            collective_id=0, has_side_effects=True, vmem_limit_bytes=48 * 2**20
        ),
        name="exchange_and_multiply",
    )(*[pltpu.with_memory_space_constraint(v, pltpu.HBM) for v in operands])


def solution(mesh):
    in_specs = (
        P(None, ("parts", "tm"), None, ("space", "spin"), None),
        P(None, None, ("parts", "tm"), None, ("space", "spin"), None),
        P(None, "parts", "spin", "space", "tm"),
        P(),
        P(),
        P(),
        P(),
    )
    out_specs = P(None, None, ("parts", "tm"), "spin", "space", None)
    run = functools.partial(local, mesh.shape["tm"], mesh.shape["space"], mesh.shape["spin"])
    return jax.shard_map(run, mesh=mesh, in_specs=in_specs, out_specs=out_specs, check_vma=False)
```
